1024 devices in a mesh: dom: 128 (over z, x_hi, core), seg: 8 (over x_lo, y).
Axes of the slice: x: 4 (x_hi: 2, x_lo: 2; x = x_hi * 2 + x_lo), y: 4, z: 32, core: 2. Of those that a mesh axis runs over, the one named last changes fastest.
Arguments:
- state: float32 [8192, 9, 64], P(('dom', 'seg'))
- counts: int32 [8192], P(('dom', 'seg')), may hold values from 16 to 64
- neighbours: int32 [8192, 26], P(('dom', 'seg')), may hold values from 0 to 191, as said below
- new_place: int32 [8192], P(('dom', 'seg')), may hold values from 0 to 63, as said below
Outputs:
- moved_state: float32 [8192, 9, 64], P(('dom', 'seg'))
- moved_density: float32 [8192, 64], P(('dom', 'seg'))
The draws below stay inside these ranges and needn't reach their ends.
Inputs may be any that keep to these rules, and one draw needn't show every extreme that they name: `neighbours`: each row lists 26 distinct region indices in 0 to 191, never the block's own index 64 + k. `new_place`: within each domain range the 64 values are a permutation.
All inputs are finite; a program needn't handle non-finite values.
Results may differ from the reference program's by a relative error of at most 0.00002.
Values sent between devices are 32-bit elements; how exact they have to be, the bound alone decides.
A program may use at most 32 MiB of HBM per device.

```python
import math
import jax
import jax.numpy as jnp
from jax import lax

P_SIZE = 64
NBR = 26
SLAB = 64
NB = 8192


def draw_state(key, part):
    keys = jax.random.split(jax.random.fold_in(key, 11), 5)
    position = jax.random.normal(keys[0], (NB, 3, P_SIZE), jnp.float32)
    velocity = 0.5 * jax.random.normal(keys[1], (NB, 3, P_SIZE), jnp.float32)
    mass = jnp.exp(jax.random.uniform(keys[2], (NB, 1, P_SIZE), jnp.float32, jnp.log(0.2), jnp.log(2.0)))
    smooth = jnp.exp(jax.random.uniform(keys[3], (NB, 1, P_SIZE), jnp.float32, jnp.log(0.6), jnp.log(1.2)))
    energy = jnp.exp(jax.random.uniform(keys[4], (NB, 1, P_SIZE), jnp.float32, jnp.log(0.2), jnp.log(3.0)))
    return jnp.concatenate([position, velocity, mass, smooth, energy], axis=1)


def draw_neighbours(key, part):
    rows = jnp.arange(NB, dtype=jnp.int32)
    region = 3 * SLAB
    scores = jax.random.randint(jax.random.fold_in(key, 23), (NB, region), 0, 1 << 20, dtype=jnp.int32)
    columns = jnp.arange(region, dtype=jnp.int32)
    scores = scores * 512 + columns[None, :]
    self_column = SLAB + rows % SLAB
    scores = jnp.where(columns[None, :] == self_column[:, None], -1, scores)
    return lax.top_k(scores, NBR)[1].astype(jnp.int32)


def draw_new_place(key, part):
    ranges = NB // SLAB
    keys = jax.random.split(jax.random.fold_in(key, 37), ranges)
    places = jax.vmap(lambda k: jax.random.permutation(k, SLAB))(keys)
    return places.reshape(-1).astype(jnp.int32)


def touch_ends(drawn, rng, smallest, high):
    longest = drawn.shape.index(max(drawn.shape))
    spots = []
    for shift in (0, 1):
        where = [jax.random.randint(jax.random.fold_in(rng, axis), (), 0, length) for axis, length in enumerate(drawn.shape)]
        where[longest] = (where[longest] + shift) % drawn.shape[longest]
        spots.append(tuple(where))
    return drawn.at[spots[0]].set(smallest).at[spots[1]].set(high)


def setup_inputs(seed: int = 0) -> dict:
    splits = jax.random.split(jax.random.key(seed), 5)
    state = draw_state(jax.random.fold_in(splits[4], 71), 0)
    counts = touch_ends(jax.random.randint(splits[1], (NB,), P_SIZE // 4, P_SIZE + 1), jax.random.fold_in(splits[1], 1), P_SIZE // 4, P_SIZE).astype(jnp.int32)
    neighbours = draw_neighbours(jax.random.fold_in(splits[4], 71), 0)
    new_place = draw_new_place(jax.random.fold_in(splits[4], 71), 0)
    return dict(state=state, counts=counts, neighbours=neighbours, new_place=new_place)


SIGMA = 21.0 / (16.0 * math.pi)
GAMMA_LESS = 2.0 / 3.0
STEP_DT = 0.1

def offsets(own_pos, far_pos):
    return own_pos[:, :, None] - far_pos[:, None, :]

def density_tile(own, far):
    diff = offsets(own[0:3], far[0:3])
    dist = jnp.sqrt(lax.optimization_barrier(jnp.sum(diff * diff, axis=0)))
    smooth = own[7][:, None]
    ratio = dist / smooth
    shell = jnp.maximum(1.0 - 0.5 * ratio, 0.0)
    kernel = SIGMA / smooth ** 3 * shell ** 4 * (1.0 + 2.0 * ratio)
    return lax.optimization_barrier(jnp.sum(kernel * far[6][None, :], axis=1))

def slope(own, far):
    diff = offsets(own[0:3], far[0:3])
    dist = jnp.sqrt(lax.optimization_barrier(jnp.sum(diff * diff, axis=0)))
    smooth = 0.5 * (own[7][:, None] + far[7][None, :])
    ratio = dist / smooth
    shell = jnp.maximum(1.0 - 0.5 * ratio, 0.0)
    factor = -5.0 * SIGMA / smooth ** 5 * shell ** 3
    return (diff, factor)

def tensor_tile(own, far, far_vol):
    diff, factor = slope(own, far)
    weight = -factor * far_vol[None, :]
    pairs = ((0, 0), (1, 1), (2, 2), (0, 1), (0, 2), (1, 2))
    return jnp.stack([lax.optimization_barrier(jnp.sum(weight * diff[a] * diff[b], axis=1)) for a, b in pairs])

def corrected(tensor):
    return jnp.stack([2.0 - tensor[0], 2.0 - tensor[1], 2.0 - tensor[2], -tensor[3], -tensor[4], -tensor[5]])

def apply_sym(sym, vec):
    first = sym[0] * vec[0] + sym[3] * vec[1] + sym[4] * vec[2]
    second = sym[3] * vec[0] + sym[1] * vec[1] + sym[5] * vec[2]
    third = sym[4] * vec[0] + sym[5] * vec[1] + sym[2] * vec[2]
    return jnp.stack([first, second, third])

def momentum_tile(own, own_corr, own_press, far, far_corr, far_press):
    diff, factor = slope(own, far)
    scaled = diff * factor[None]
    grad_own = apply_sym(own_corr[:, :, None], scaled)
    grad_far = apply_sym(far_corr[:, None, :], scaled)
    mass_far = far[6][None, :]
    accel = -lax.optimization_barrier(jnp.sum(mass_far[None] * (own_press[None, :, None] * grad_own + far_press[None, None, :] * grad_far), axis=2))
    dvel = own[3:6][:, :, None] - far[3:6][:, None, :]
    heat = own_press * lax.optimization_barrier(jnp.sum(mass_far * lax.optimization_barrier(jnp.sum(dvel * grad_own, axis=0)), axis=1))
    return (accel, heat)

def tile_of(padded, index):
    tile = padded[index]
    if tile.ndim == 3:
        return jnp.moveaxis(tile, 0, 1).reshape(tile.shape[1], -1)
    return tile.reshape(-1)

def reference(state, counts, neighbours, new_place):
    total = state.shape[0]
    width = state.shape[2]
    live = (jnp.arange(width, dtype=jnp.int32)[None, :] < counts[:, None]).astype(jnp.float32)
    base = jnp.concatenate([state[:, 0:6], (state[:, 6] * live)[:, None], state[:, 7:9]], axis=1)
    rows = jnp.arange(total, dtype=jnp.int32)
    lists = jnp.concatenate([(SLAB + rows % SLAB)[:, None], neighbours], axis=1)
    glob = ((rows // SLAB)[:, None] * SLAB + lists).astype(jnp.int32)

    def pad(values):
        zeros = jnp.zeros((SLAB,) + values.shape[1:], values.dtype)
        return jnp.concatenate([zeros, values, zeros], axis=0)
    padded_state = pad(base)

    def first(r):
        return density_tile(base[r], tile_of(padded_state, glob[r]))
    rho = lax.map(first, rows) + (1.0 - live)
    vol = base[:, 6] / rho
    padded_vol = pad(vol)

    def second(r):
        return tensor_tile(base[r], tile_of(padded_state, glob[r]), tile_of(padded_vol, glob[r]))
    corr = corrected(jnp.moveaxis(lax.map(second, rows), 1, 0))
    corr = jnp.moveaxis(corr, 0, 1)
    press = GAMMA_LESS * base[:, 8] / rho
    extra = jnp.concatenate([corr, press[:, None]], axis=1)
    padded_extra = pad(extra)

    def third(r):
        far_extra = tile_of(padded_extra, glob[r])
        return momentum_tile(base[r], corr[r], press[r], tile_of(padded_state, glob[r]), far_extra[0:6], far_extra[6])
    accel, heat = lax.map(third, rows)
    accel = accel * live[:, None]
    heat = heat * live
    velocity = state[:, 3:6] + STEP_DT * accel
    position = state[:, 0:3] + STEP_DT * velocity
    energy = state[:, 8] + STEP_DT * heat
    updated = jnp.concatenate([position, velocity, state[:, 6:8], energy[:, None]], axis=1)
    dest = (rows // SLAB * SLAB + new_place).astype(jnp.int32)
    moved_state = jnp.zeros_like(updated).at[dest].set(updated)
    moved_density = jnp.zeros_like(rho).at[dest].set(rho)
    return (moved_state, moved_density)
```

```python
import functools
import math

import jax
import jax.numpy as jnp
from jax import lax
from jax.experimental import pallas as pl
from jax.experimental.pallas import tpu as pltpu
from jax.sharding import PartitionSpec as P

SIGMA = 21.0 / (16.0 * math.pi)
SLOPE = -5.0 * 32.0 * SIGMA
GAMMA_LESS = 2.0 / 3.0
STEP_DT = 0.1
MESH = pl.DeviceIdType.MESH
F32 = jnp.float32
BF16 = jnp.bfloat16
SPLITS = 3
TINY = 1e-36


def split(value):
    parts = []
    for k in range(SPLITS):
        part = value.astype(BF16)
        parts.append(part)
        if k + 1 < SPLITS:
            value = value - part.astype(F32)
    return parts


def kernel(
    dims,
    state_ref,
    nb_ref,
    counts_ref,
    place_ref,
    out_ref,
    rho_ref,
    meta,
    pack_a,
    pack_b,
    pack_c,
    reg_m,
    reg_a,
    reg_b,
    reg_c,
    table,
    table_smem,
    far,
    far1,
    own_wide,
    weights,
    own_e,
    sums,
    res_l,
    res_m,
    res_q,
    moment,
    copy_sem,
    send_m,
    recv_m,
    send_a,
    recv_a,
    send_b,
    recv_b,
    send_c,
    recv_c,
):
    D, G, NBR = dims
    B = 8
    HALF = B // 2
    W = 64
    SLAB = G * B
    TILES = (NBR + 2) // 2
    SELF, PAD, PLACE, COUNT, TABLE0 = NBR, NBR + 1, 28, 29, 64
    dom = lax.axis_index("dom")
    seg = lax.axis_index("seg")

    def target(delta, o):
        return (lax.rem(dom + delta + D, D), lax.rem(seg + o, G))

    def each_peer(action):
        for delta in (-1, 1):

            def outer(o, c, delta=delta):
                action(delta, o)
                return c

            lax.fori_loop(0, G, outer, 0)

        def inner(o, c):
            action(0, o)
            return c

        lax.fori_loop(1, G, inner, 0)

    barrier = pltpu.get_barrier_semaphore()

    def greet(delta, o):
        pl.semaphore_signal(barrier, inc=1, device_id=target(delta, o), device_id_type=MESH)

    each_peer(greet)

    rows = lax.broadcasted_iota(jnp.int32, (B, 128), 0)
    lanes = lax.broadcasted_iota(jnp.int32, (B, 128), 1)
    low = lanes < W

    note = jnp.where(lanes == SELF, SLAB + seg * B + rows, 0)
    note = jnp.where(lanes == PAD, 3 * SLAB, note)
    for b in range(B):
        mine = rows == b
        note = jnp.where(mine & (lanes == PLACE), place_ref[b], note)
        note = jnp.where(mine & (lanes == COUNT), counts_ref[b], note)
        note = jnp.where((rows == 0) & (lanes == TABLE0 + seg * B + b), place_ref[b], note)
    meta[...] = note
    meta[:, 0:NBR] = nb_ref[...]
    for p in range(HALF):
        pair = jnp.concatenate([state_ref[p, 0:8, :], state_ref[p + HALF, 0:8, :]], axis=1)
        limit = jnp.where(low, counts_ref[p], counts_ref[p + HALF] + W)
        pack_a[p] = jnp.where((rows == 6) & (lanes >= limit), 0.0, pair)
        pack_a[HALF, p : p + 1] = jnp.concatenate(
            [state_ref[p, 8:9, :], state_ref[p + HALF, 8:9, :]], axis=1
        )
        pack_a[HALF, p + HALF : p + HALF + 1] = jnp.concatenate(
            [state_ref[p, 6:7, :], state_ref[p + HALF, 6:7, :]], axis=1
        )

    pl.semaphore_wait(barrier, 3 * G - 1)

    def sent(src, dst, send_sem, recv_sem):
        def make(delta, o):
            slot = (1 - delta) * G + seg
            return pltpu.make_async_remote_copy(
                src_ref=src(delta),
                dst_ref=dst(slot, delta),
                send_sem=send_sem.at[(1 + delta) * G + o],
                recv_sem=recv_sem.at[slot],
                device_id=target(delta, o),
                device_id_type=MESH,
            )

        def take(delta, o):
            slot = (1 + delta) * G + lax.rem(seg + o, G)
            return pltpu.make_async_remote_copy(
                src_ref=src(delta),
                dst_ref=dst(slot, delta),
                send_sem=send_sem.at[(1 + delta) * G + o],
                recv_sem=recv_sem.at[slot],
                device_id=target(delta, o),
                device_id_type=MESH,
            )

        return (
            lambda: each_peer(lambda delta, o: make(delta, o).start()),
            lambda: each_peer(lambda delta, o: take(delta, o).wait_recv()),
            lambda: each_peer(lambda delta, o: make(delta, o).wait_send()),
        )

    meta_go, meta_in, meta_out = sent(
        lambda d: meta, lambda s, d: reg_m.at[s], send_m, recv_m
    )
    a_go, a_in, a_out = sent(
        lambda d: pack_a if d == 0 else pack_a.at[0:HALF],
        lambda s, d: reg_a.at[s] if d == 0 else reg_a.at[s, 0:HALF],
        send_a,
        recv_a,
    )
    b_go, b_in, b_out = sent(lambda d: pack_b, lambda s, d: reg_b.at[s], send_b, recv_b)
    c_go, c_in, c_out = sent(lambda d: pack_c, lambda s, d: reg_c.at[s], send_c, recv_c)

    meta_go()
    a_go()

    here = G + seg
    reg_m[here] = meta[...]
    reg_a[here] = pack_a[...]
    none = 3 * G
    zero = jnp.zeros((8, 128), F32)
    reg_b[none] = zero
    for p in range(HALF):
        reg_a[none, p] = zero
        reg_c[none, p] = zero
    reg_a[none, HALF] = zero

    meta_in()
    lists = jnp.zeros((B, 128), jnp.int32)
    notes = [reg_m[G + d] for d in range(G)]
    places = [jnp.broadcast_to(note[:, PLACE : PLACE + 1], (B, 128)) for note in notes]
    for b in range(B):
        found = jnp.zeros((B, 128), jnp.int32)
        for d in range(G):
            found = found + jnp.where(places[d] == seg * B + b, notes[d], 0)
        for shift in (4, 2, 1):
            found = found + pltpu.roll(found, shift, 0)
        lists = jnp.where(rows == b, found, lists)
    spread = []
    for q in range(3):
        total = reg_m[q * G, 0:1, :]
        for d in range(1, G):
            total = total + reg_m[q * G + d, 0:1, :]
        total = jnp.broadcast_to(total, (B, 128))
        spread.append(jnp.where(low, pltpu.roll(total, W, 1), total))
    first = jnp.where(low, spread[0], spread[1]) if SLAB == W else None
    if SLAB == W:
        inside = lists & 127
        placed = jnp.where(
            lists < 128,
            jnp.take_along_axis(first, inside, axis=1, mode="promise_in_bounds"),
            jnp.take_along_axis(spread[2], inside, axis=1, mode="promise_in_bounds"),
        )
        moved = jnp.where(lists < 3 * SLAB, (lists & (-SLAB)) + placed, lists)
    else:
        moved = lists
        inside = lists & (SLAB - 1)
        for q in range(3):
            got = jnp.take_along_axis(spread[q], inside, axis=1, mode="promise_in_bounds")
            moved = jnp.where((lists >= q * SLAB) & (lists < (q + 1) * SLAB), q * SLAB + got, moved)
    inside = jnp.clip(lists, 0, 3 * SLAB)
    moved = jnp.clip(moved, 0, 3 * SLAB)
    half = (inside >> 2) & 1
    table[0] = (((inside >> 3) * (HALF + 1) + (inside & 3)) << 1) | half
    table[1] = (((moved >> 3) * HALF + (moved & 3)) << 1) | ((moved >> 2) & 1)
    live = jnp.where(lanes < jnp.broadcast_to(lists[:, COUNT : COUNT + 1], (B, 128)), 1.0, 0.0)
    to_smem = pltpu.make_async_copy(table, table_smem, copy_sem)
    to_smem.start()
    to_smem.wait()

    a_in()

    @pl.when(dom == 0)
    def _():
        for d in range(G):
            for p in range(HALF):
                reg_a[d, p] = zero

    @pl.when(dom == D - 1)
    def _():
        for d in range(G):
            for p in range(HALF):
                reg_a[2 * G + d, p] = zero

    def joined(which, b, t, load):
        even, odd = table_smem[which, b, 2 * t], table_smem[which, b, 2 * t + 1]
        left, right = load(even >> 1), load(odd >> 1)
        left = pltpu.roll(left, (even & 1) * W, 1)
        right = pltpu.roll(right, W - (odd & 1) * W, 1)
        mask = low if left.shape[0] == B else low[0:1]
        return jnp.where(mask, left, right)

    def load_a(tile):
        return reg_a[lax.div(tile, HALF + 1), lax.rem(tile, HALF + 1)]

    def load_b(row):
        return reg_b[row >> 2, pl.ds(row & 3, 1), :]

    def load_c(tile):
        return reg_c[tile >> 2, tile & 3]

    def density(b, c):
        own = joined(0, b, TILES - 1, load_a)
        where_own = table_smem[0, b, SELF]
        dev, pair = lax.div(where_own >> 1, HALF + 1), lax.rem(where_own >> 1, HALF + 1)
        shift = (where_own & 1) * W
        own_e[pl.ds(b, 1), :] = pltpu.roll(reg_a[dev, HALF, pl.ds(pair, 1), :], shift, 1)
        own_e[pl.ds(B + b, 1), :] = pltpu.roll(
            reg_a[dev, HALF, pl.ds(HALF + pair, 1), :], shift, 1
        )
        centre = jnp.sum(jnp.where(low, own, 0.0), axis=1, keepdims=True) * (1.0 / W)
        centre = jnp.where(rows < 6, jnp.broadcast_to(centre, (B, 128)), 0.0)
        turned = jnp.transpose(own)[0:W]
        for k, field in enumerate((0, 1, 2, 7)):
            own_wide[k] = jnp.broadcast_to(turned[:, field : field + 1], (W, 128))
        own_wide[4] = 0.5 / own_wide[3]

        def tile(t, acc):
            value = joined(0, b, t, load_a)
            far[pl.ds(pl.multiple_of((b * TILES + t) * 8, 8), 8), :] = value
            far1[pl.ds(pl.multiple_of((b * TILES + t) * 8, 8), 8), :] = jnp.where(
                rows == 6, 1.0, value - centre
            )
            fx, fy, fz = value[0:1], value[1:2], value[2:3]
            fm, fh = value[6:7], value[7:8]
            at = pl.ds(pl.multiple_of(t * 128, 128), 128)
            new = []
            for g in range(W // 16):
                part = pl.ds(g * 16, 16)
                dx = own_wide[0, part, :] - fx
                dy = own_wide[1, part, :] - fy
                dz = own_wide[2, part, :] - fz
                square = jnp.maximum(dx * dx + dy * dy + dz * dz, TINY)
                dist = square * lax.rsqrt(square)
                q = dist * own_wide[4, part, :]
                shell = jnp.maximum(1.0 - q, 0.0)
                shell = shell * shell
                kern = shell * shell * (1.0 + 4.0 * q)
                new.append(acc[g * 16 : g * 16 + 16] + kern * fm)
                inv = 1.0 / (own_wide[3, part, :] + fh)
                shell = jnp.maximum(1.0 - dist * inv, 0.0) * inv
                shell2 = shell * shell
                factor = (shell * (inv * inv)) * shell2
                for k, piece in enumerate(split(factor)):
                    weights[k, b, part, at] = piece
            return jnp.concatenate(new, axis=0)

        acc = lax.fori_loop(0, TILES, tile, jnp.zeros((W, 128), F32))
        sums[pl.ds(b, 1), 0:W] = jnp.sum(jnp.transpose(acc), axis=0, keepdims=True)
        return c

    lax.fori_loop(0, B, density, 0)

    def own_field(ref, k):
        return ref[pl.ds((TILES - 1) * 8 + k, B, stride=TILES * 8), :]

    mass, smooth = own_field(far, 6), own_field(far, 7)
    xi = [own_field(far1, k) for k in range(3)]
    vi = [own_field(far1, 3 + k) for k in range(3)]
    rho = SIGMA / (smooth * smooth * smooth) * sums[...] + (1.0 - live)
    rho = jnp.where(low, rho, 1.0)
    vol = mass / rho
    press = GAMMA_LESS * own_e[0:B] / rho
    rho_ref[...] = rho[:, 0:W]

    def packed(value):
        return jnp.concatenate([value[0:HALF, 0:W], value[HALF:B, 0:W]], axis=1)

    pack_b[0:HALF, :] = packed(vol)
    pack_b[HALF:B, :] = jnp.zeros((HALF, 128), F32)
    b_go()
    reg_b[here] = pack_b[...]

    def store_moment(k, t, value):
        at = pl.ds(pl.multiple_of(t * 128, 128), 128)
        for s, piece in enumerate(split(value)):
            moment[pl.ds(s * 32 + k * 16, 16), at] = piece

    def store_products(t, tile, by):
        store_moment(0, t, jnp.concatenate([tile, tile * by[0:1]], axis=0))
        store_moment(1, t, jnp.concatenate([tile * by[1:2], tile * by[2:3]], axis=0))

    def summed(b, out):
        total = None
        for k in range(SPLITS):
            got = lax.dot_general(
                moment[0 : 32 * (SPLITS - k), :],
                weights[k, b],
                (((1,), (1,)), ((), ())),
                preferred_element_type=F32,
            )
            for s in range(SPLITS - k):
                piece = got[32 * s : 32 * s + 32]
                total = piece if total is None else total + piece
        out[pl.ds(pl.multiple_of(b * 32, 32), 32), 0:W] = total

    def far1_tile(b, t):
        return far1[pl.ds(pl.multiple_of((b * TILES + t) * 8, 8), 8), :]

    def field(ref, k):
        return ref[pl.ds(k, B, stride=32), :]

    def masses(b, c):
        def tile(t, c):
            value = far1_tile(b, t)
            fm = far[pl.ds((b * TILES + t) * 8 + 6, 1), :]
            store_products(t, value * fm, value)
            return c

        lax.fori_loop(0, TILES, tile, 0)
        summed(b, res_m)
        return c

    lax.fori_loop(0, B, masses, 0)

    b_in()

    @pl.when(dom == 0)
    def _():
        for d in range(G):
            reg_b[d] = zero

    @pl.when(dom == D - 1)
    def _():
        for d in range(G):
            reg_b[2 * G + d] = zero

    def tensor(b, c):
        def tile(t, c):
            value = far1_tile(b, t)
            store_products(t, value * joined(1, b, t, load_b), value)
            return c

        lax.fori_loop(0, TILES, tile, 0)
        summed(b, res_l)
        return c

    lax.fori_loop(0, B, tensor, 0)

    s0 = field(res_l, 6)
    s1 = [field(res_l, k) for k in range(3)]
    pairs = ((0, 0), (1, 1), (2, 2), (0, 1), (0, 2), (1, 2))
    corr = []
    for a, b in pairs:
        value = s0 * xi[a] * xi[b] - xi[a] * s1[b] - xi[b] * s1[a] + field(res_l, 8 + 8 * a + b)
        corr.append((2.0 if a == b else 0.0) + SLOPE * value)
    scale = mass * press
    for k in range(6):
        pack = packed(scale * corr[k])
        for p in range(HALF):
            pack_c[p, k : k + 1, :] = pack[p : p + 1]
    for p in range(HALF):
        pack_c[p, 6:8, :] = jnp.zeros((2, 128), F32)
    c_go()
    for p in range(HALF):
        reg_c[here, p] = pack_c[p]

    a0 = field(res_m, 6)
    a1 = [field(res_m, k) for k in range(3)]
    v1 = [field(res_m, 3 + k) for k in range(3)]
    at = ((0, 3, 4), (3, 1, 5), (4, 5, 2))
    grad = [a0 * xi[a] - a1[a] for a in range(3)]
    pull = []
    heat = None
    for a in range(3):
        row = [corr[at[a][b]] for b in range(3)]
        pull.append(press * (row[0] * grad[0] + row[1] * grad[1] + row[2] * grad[2]))
        for b in range(3):
            work = vi[a] * grad[b] - v1[a] * xi[b] + field(res_m, 8 + 8 * b + 3 + a)
            term = row[b] * work
            heat = term if heat is None else heat + term
    energy = own_e[0:B] + STEP_DT * SLOPE * (live * press * heat)

    c_in()

    @pl.when(dom == 0)
    def _():
        for d in range(G):
            for p in range(HALF):
                reg_c[d, p] = zero

    @pl.when(dom == D - 1)
    def _():
        for d in range(G):
            for p in range(HALF):
                reg_c[2 * G + d, p] = zero

    def momentum(b, c):
        def tile(t, c):
            store_products(t, joined(1, b, t, load_c), far1_tile(b, t))
            return c

        lax.fori_loop(0, TILES, tile, 0)
        summed(b, res_q)
        return c

    lax.fori_loop(0, B, momentum, 0)

    for a in range(3):
        far_sum = None
        for b in range(3):
            k = at[a][b]
            term = field(res_q, k) * xi[b] - field(res_q, 8 + 8 * b + k)
            far_sum = term if far_sum is None else far_sum + term
        accel = (-SLOPE) * live * (pull[a] + far_sum)
        velocity = own_field(far, 3 + a) + STEP_DT * accel
        position = own_field(far, a) + STEP_DT * velocity
        out_ref[:, a, :] = position[:, 0:W]
        out_ref[:, 3 + a, :] = velocity[:, 0:W]
    out_ref[:, 6, :] = own_e[B : 2 * B, 0:W]
    out_ref[:, 7, :] = smooth[:, 0:W]
    out_ref[:, 8, :] = energy[:, 0:W]

    meta_out()
    a_out()
    b_out()
    c_out()


def local(sizes, state, counts, neighbours, new_place):
    D, G = sizes
    blocks, _, width = state.shape
    NBR = neighbours.shape[1]
    tiles = (NBR + 2) // 2
    half = blocks // 2
    vmem = pl.BlockSpec(memory_space=pltpu.VMEM)
    smem = pl.BlockSpec(memory_space=pltpu.SMEM)
    sems = pltpu.SemaphoreType.DMA((3 * G,))
    return pl.pallas_call(
        functools.partial(kernel, (D, G, NBR)),
        out_shape=(
            jax.ShapeDtypeStruct(state.shape, F32),
            jax.ShapeDtypeStruct((blocks, width), F32),
        ),
        in_specs=[vmem, vmem, smem, smem],
        out_specs=(vmem, vmem),
        scratch_shapes=[
            pltpu.VMEM((8, 128), jnp.int32),
            pltpu.VMEM((half + 1, 8, 128), F32),
            pltpu.VMEM((8, 128), F32),
            pltpu.VMEM((half, 8, 128), F32),
            pltpu.VMEM((3 * G, 8, 128), jnp.int32),
            pltpu.VMEM((3 * G + 1, half + 1, 8, 128), F32),
            pltpu.VMEM((3 * G + 1, 8, 128), F32),
            pltpu.VMEM((3 * G + 1, half, 8, 128), F32),
            pltpu.VMEM((2, 8, 128), jnp.int32),
            pltpu.SMEM((2, 8, 128), jnp.int32),
            pltpu.VMEM((blocks * tiles * 8, 128), F32),
            pltpu.VMEM((blocks * tiles * 8, 128), F32),
            pltpu.VMEM((5, width, 128), F32),
            pltpu.VMEM((SPLITS, blocks, width, tiles * 128), BF16),
            pltpu.VMEM((16, 128), F32),
            pltpu.VMEM((8, 128), F32),
            pltpu.VMEM((blocks * 32, 128), F32),
            pltpu.VMEM((blocks * 32, 128), F32),
            pltpu.VMEM((blocks * 32, 128), F32),
            pltpu.VMEM((SPLITS * 32, tiles * 128), BF16),
            pltpu.SemaphoreType.DMA,
        ]
        + [sems] * 8,
        compiler_params=pltpu.CompilerParams(
            collective_id=0, has_side_effects=True, vmem_limit_bytes=40 * 2**20
        ),
    )(state, neighbours, counts, new_place)


def solution(mesh):
    sizes = (mesh.shape["dom"], mesh.shape["seg"])
    both = ("dom", "seg")
    return jax.shard_map(
        functools.partial(local, sizes),
        mesh=mesh,
        in_specs=(P(both, None, None), P(both), P(both, None), P(both)),
        out_specs=(P(both, None, None), P(both, None)),
        check_vma=False,
    )
```

```python
import functools
import math

import jax
import jax.numpy as jnp
from jax import lax
from jax.experimental import pallas as pl
from jax.experimental.pallas import tpu as pltpu
from jax.sharding import PartitionSpec as P

SIGMA = 21.0 / (16.0 * math.pi)
SLOPE = -5.0 * 32.0 * SIGMA
GAMMA_LESS = 2.0 / 3.0
STEP_DT = 0.1
MESH = pl.DeviceIdType.MESH
F32 = jnp.float32
BF16 = jnp.bfloat16
SPLITS = 3
TINY = 1e-36


def split(value):
    parts = []
    for k in range(SPLITS):
        part = value.astype(BF16)
        parts.append(part)
        if k + 1 < SPLITS:
            value = value - part.astype(F32)
    return parts


def kernel(
    dims,
    state_ref,
    nb_ref,
    counts_ref,
    place_ref,
    out_ref,
    rho_ref,
    meta,
    pack_a,
    pack_b,
    pack_c,
    reg_m,
    reg_a,
    reg_b,
    reg_c,
    table,
    table_smem,
    far,
    far1,
    own_wide,
    smooth_wide,
    dists,
    weights,
    own_e,
    sums,
    res_l,
    res_m,
    res_q,
    moment,
    copy_sem,
    send_m,
    recv_m,
    send_a,
    recv_a,
    send_b,
    recv_b,
    send_c,
    recv_c,
):
    D, G, NBR = dims
    B = 8
    HALF = B // 2
    W = 64
    SLAB = G * B
    TILES = (NBR + 2) // 2
    SELF, PAD, PLACE, COUNT, TABLE0 = NBR, NBR + 1, 28, 29, 64
    dom = lax.axis_index("dom")
    seg = lax.axis_index("seg")

    def wrapped(value, size):
        return value & (size - 1) if size & (size - 1) == 0 else lax.rem(value, size)

    def target(delta, o):
        return (wrapped(dom + delta + D, D), wrapped(seg + o, G))

    def each_peer(action):
        for delta in (-1, 1):

            def outer(o, c, delta=delta):
                action(delta, o)
                return c

            lax.fori_loop(0, G, outer, 0, unroll=True)

        def inner(o, c):
            action(0, o)
            return c

        lax.fori_loop(1, G, inner, 0, unroll=True)

    barrier = pltpu.get_barrier_semaphore()

    def greet(delta, o):
        pl.semaphore_signal(barrier, inc=1, device_id=target(delta, o), device_id_type=MESH)

    each_peer(greet)

    rows = lax.broadcasted_iota(jnp.int32, (B, 128), 0)
    lanes = lax.broadcasted_iota(jnp.int32, (B, 128), 1)
    low = lanes < W

    note = jnp.where(lanes == SELF, SLAB + seg * B + rows, 0)
    note = jnp.where(lanes == PAD, 3 * SLAB, note)
    for b in range(B):
        mine = rows == b
        note = jnp.where(mine & (lanes == PLACE), place_ref[b], note)
        note = jnp.where(mine & (lanes == COUNT), counts_ref[b], note)
        note = jnp.where((rows == 0) & (lanes == TABLE0 + seg * B + b), place_ref[b], note)
    meta[...] = note
    meta[:, 0:NBR] = nb_ref[...]
    for p in range(HALF):
        pair = jnp.concatenate(
            [state_ref[pl.ds(q, 8, stride=B), :] for q in (p, p + HALF)], axis=1
        )
        limit = jnp.where(low, counts_ref[p], counts_ref[p + HALF] + W)
        pack_a[p] = jnp.where((rows == 6) & (lanes >= limit), 0.0, pair)
    for k, f in enumerate((8, 6)):
        pack_a[HALF, k * HALF : k * HALF + HALF] = jnp.concatenate(
            [state_ref[f * B + h * HALF : f * B + h * HALF + HALF, :] for h in (0, 1)], axis=1
        )

    pl.semaphore_wait(barrier, 3 * G - 1)

    def sent(src, dst, send_sem, recv_sem):
        def make(delta, o):
            slot = (1 - delta) * G + seg
            return pltpu.make_async_remote_copy(
                src_ref=src(delta),
                dst_ref=dst(slot, delta),
                send_sem=send_sem.at[(1 + delta) * G + o],
                recv_sem=recv_sem.at[slot],
                device_id=target(delta, o),
                device_id_type=MESH,
            )

        def take(delta, o):
            slot = (1 + delta) * G + wrapped(seg + o, G)
            return pltpu.make_async_remote_copy(
                src_ref=src(delta),
                dst_ref=dst(slot, delta),
                send_sem=send_sem.at[(1 + delta) * G + o],
                recv_sem=recv_sem.at[slot],
                device_id=target(delta, o),
                device_id_type=MESH,
            )

        return (
            lambda: each_peer(lambda delta, o: make(delta, o).start()),
            lambda: each_peer(lambda delta, o: take(delta, o).wait_recv()),
            lambda: each_peer(lambda delta, o: make(delta, o).wait_send()),
        )

    meta_go, meta_in, meta_out = sent(
        lambda d: meta, lambda s, d: reg_m.at[s], send_m, recv_m
    )
    a_go, a_in, a_out = sent(
        lambda d: pack_a if d == 0 else pack_a.at[0:HALF],
        lambda s, d: reg_a.at[s] if d == 0 else reg_a.at[s, 0:HALF],
        send_a,
        recv_a,
    )
    b_go, b_in, b_out = sent(lambda d: pack_b, lambda s, d: reg_b.at[s], send_b, recv_b)
    c_go, c_in, c_out = sent(lambda d: pack_c, lambda s, d: reg_c.at[s], send_c, recv_c)

    meta_go()
    a_go()

    here = G + seg
    reg_m[here] = meta[...]
    reg_a[here] = pack_a[...]
    none = 3 * G
    zero = jnp.zeros((8, 128), F32)
    reg_b[none] = zero
    for p in range(HALF):
        reg_a[none, p] = zero
        reg_c[none, p] = zero
    reg_a[none, HALF] = zero

    meta_in()
    lists = jnp.zeros((B, 128), jnp.int32)
    notes = [reg_m[G + d] for d in range(G)]
    places = [jnp.broadcast_to(note[:, PLACE : PLACE + 1], (B, 128)) for note in notes]
    for b in range(B):
        found = jnp.zeros((B, 128), jnp.int32)
        for d in range(G):
            found = found + jnp.where(places[d] == seg * B + b, notes[d], 0)
        for shift in (4, 2, 1):
            found = found + pltpu.roll(found, shift, 0)
        lists = jnp.where(rows == b, found, lists)
    spread = []
    for q in range(3):
        total = reg_m[q * G, 0:1, :]
        for d in range(1, G):
            total = total + reg_m[q * G + d, 0:1, :]
        total = jnp.broadcast_to(total, (B, 128))
        spread.append(jnp.where(low, pltpu.roll(total, W, 1), total))
    first = jnp.where(low, spread[0], spread[1]) if SLAB == W else None
    if SLAB == W:
        inside = lists & 127
        placed = jnp.where(
            lists < 128,
            jnp.take_along_axis(first, inside, axis=1, mode="promise_in_bounds"),
            jnp.take_along_axis(spread[2], inside, axis=1, mode="promise_in_bounds"),
        )
        moved = jnp.where(lists < 3 * SLAB, (lists & (-SLAB)) + placed, lists)
    else:
        moved = lists
        inside = lists & (SLAB - 1)
        for q in range(3):
            got = jnp.take_along_axis(spread[q], inside, axis=1, mode="promise_in_bounds")
            moved = jnp.where((lists >= q * SLAB) & (lists < (q + 1) * SLAB), q * SLAB + got, moved)
    inside = jnp.clip(lists, 0, 3 * SLAB)
    moved = jnp.clip(moved, 0, 3 * SLAB)
    half = (inside >> 2) & 1
    table[0] = (((inside >> 3) * (HALF + 1) + (inside & 3)) << 1) | half
    table[1] = (((moved >> 3) * HALF + (moved & 3)) << 1) | ((moved >> 2) & 1)
    live = jnp.where(lanes < jnp.broadcast_to(lists[:, COUNT : COUNT + 1], (B, 128)), 1.0, 0.0)
    to_smem = pltpu.make_async_copy(table, table_smem, copy_sem)
    to_smem.start()
    to_smem.wait()

    a_in()

    @pl.when(dom == 0)
    def _():
        for d in range(G):
            for p in range(HALF):
                reg_a[d, p] = zero

    @pl.when(dom == D - 1)
    def _():
        for d in range(G):
            for p in range(HALF):
                reg_a[2 * G + d, p] = zero

    def joined(which, b, t, load):
        even, odd = table_smem[which, b, 2 * t], table_smem[which, b, 2 * t + 1]
        left, right = load(even >> 1), load(odd >> 1)
        left = pltpu.roll(left, (even & 1) * W, 1)
        right = pltpu.roll(right, W - (odd & 1) * W, 1)
        mask = low if left.shape[0] == B else low[0:1]
        return jnp.where(mask, left, right)

    def load_a(tile):
        return reg_a[lax.div(tile, HALF + 1), lax.rem(tile, HALF + 1)]

    def load_b(row):
        return reg_b[row >> 2, pl.ds(row & 3, 1), :]

    def load_c(tile):
        return reg_c[tile >> 2, tile & 3]

    def density(b, c):
        own = joined(0, b, TILES - 1, load_a)
        where_own = table_smem[0, b, SELF]
        dev, pair = lax.div(where_own >> 1, HALF + 1), lax.rem(where_own >> 1, HALF + 1)
        shift = (where_own & 1) * W
        own_e[pl.ds(b, 1), :] = pltpu.roll(reg_a[dev, HALF, pl.ds(pair, 1), :], shift, 1)
        own_e[pl.ds(B + b, 1), :] = pltpu.roll(
            reg_a[dev, HALF, pl.ds(HALF + pair, 1), :], shift, 1
        )
        centre = jnp.sum(jnp.where(low, own, 0.0), axis=1, keepdims=True) * (1.0 / W)
        centre = jnp.where(rows < 6, jnp.broadcast_to(centre, (B, 128)), 0.0)
        turned = jnp.transpose(own)[0:W]
        for k, field in enumerate((0, 1, 2, 7)):
            own_wide[k] = jnp.broadcast_to(turned[:, field : field + 1], (W, 128))
        smooth_wide[b] = own_wide[3]
        own_wide[3] = 0.5 / own_wide[3]

        def tile(t, acc):
            value = joined(0, b, t, load_a)
            far[pl.ds(pl.multiple_of((b * TILES + t) * 8, 8), 8), :] = value
            far1[pl.ds(pl.multiple_of((b * TILES + t) * 8, 8), 8), :] = jnp.where(
                rows == 6, 1.0, value - centre
            )
            fx, fy, fz = value[0:1], value[1:2], value[2:3]
            fm = value[6:7]
            at = pl.ds(pl.multiple_of(t * 128, 128), 128)
            new = []
            for g in range(W // 16):
                part = pl.ds(g * 16, 16)
                dx = own_wide[0, part, :] - fx
                dy = own_wide[1, part, :] - fy
                dz = own_wide[2, part, :] - fz
                square = jnp.maximum(dx * dx + dy * dy + dz * dz, TINY)
                dist = square * lax.rsqrt(square)
                q = dist * own_wide[3, part, :]
                shell = jnp.maximum(1.0 - q, 0.0)
                shell = shell * shell
                kern = shell * shell * (1.0 + 4.0 * q)
                new.append(acc[g * 16 : g * 16 + 16] + kern * fm)
                dists[b, part, at] = dist
            return jnp.concatenate(new, axis=0)

        acc = lax.fori_loop(0, TILES, tile, jnp.zeros((W, 128), F32), unroll=TILES)
        sums[pl.ds(b, 1), 0:W] = jnp.sum(jnp.transpose(acc), axis=0, keepdims=True)
        return c

    lax.fori_loop(0, B, density, 0)

    def own_field(ref, k):
        return ref[pl.ds((TILES - 1) * 8 + k, B, stride=TILES * 8), :]

    mass, smooth = own_field(far, 6), own_field(far, 7)
    xi = [own_field(far1, k) for k in range(3)]
    vi = [own_field(far1, 3 + k) for k in range(3)]
    rho = SIGMA / (smooth * smooth * smooth) * sums[...] + (1.0 - live)
    rho = jnp.where(low, rho, 1.0)
    vol = mass / rho
    press = GAMMA_LESS * own_e[0:B] / rho
    rho_ref[...] = rho[:, 0:W]

    def packed(value):
        return jnp.concatenate([value[0:HALF, 0:W], value[HALF:B, 0:W]], axis=1)

    pack_b[0:HALF, :] = packed(vol)
    pack_b[HALF:B, :] = jnp.zeros((HALF, 128), F32)
    b_go()
    reg_b[here] = pack_b[...]

    def blocks_of(body):
        def several(i, c):
            for k in range(4):
                body(i * 4 + k, k)
            return c

        lax.fori_loop(0, B // 4, several, 0)

    def store_moment(k, t, value, way):
        at = pl.ds(pl.multiple_of(t * 128, 128), 128)
        for s, piece in enumerate(split(value)):
            moment[way, pl.ds(s * 32 + k * 16, 16), at] = piece

    def store_products(t, tile, by, way):
        store_moment(0, t, jnp.concatenate([tile, tile * by[0:1]], axis=0), way)
        store_moment(1, t, jnp.concatenate([tile * by[1:2], tile * by[2:3]], axis=0), way)

    def summed(b, out, way):
        total = None
        for k in range(SPLITS):
            got = lax.dot_general(
                moment[way, 0 : 32 * (SPLITS - k), :],
                weights[k, b],
                (((1,), (1,)), ((), ())),
                preferred_element_type=F32,
            )
            for s in range(SPLITS - k):
                piece = got[32 * s : 32 * s + 32]
                total = piece if total is None else total + piece
        out[pl.ds(pl.multiple_of(b * 32, 32), 32), 0:W] = total

    def far1_tile(b, t):
        return far1[pl.ds(pl.multiple_of((b * TILES + t) * 8, 8), 8), :]

    def field(ref, k):
        return ref[pl.ds(k, B, stride=32), :]

    def slopes(b, c):
        def tile(t, c):
            fh = far[pl.ds((b * TILES + t) * 8 + 7, 1), :]
            at = pl.ds(pl.multiple_of(t * 128, 128), 128)
            for g in range(W // 16):
                part = pl.ds(g * 16, 16)
                inv = 1.0 / (smooth_wide[b, part, :] + fh)
                shell = jnp.maximum(1.0 - dists[b, part, at] * inv, 0.0) * inv
                shell2 = shell * shell
                factor = (shell * (inv * inv)) * shell2
                for k, piece in enumerate(split(factor)):
                    weights[k, b, part, at] = piece
            return c

        lax.fori_loop(0, TILES, tile, 0, unroll=TILES)
        return c

    lax.fori_loop(0, B, slopes, 0)

    b_in()

    @pl.when(dom == 0)
    def _():
        for d in range(G):
            reg_b[d] = zero

    @pl.when(dom == D - 1)
    def _():
        for d in range(G):
            reg_b[2 * G + d] = zero

    def tensor(b, way):
        def tile(t, c):
            value = far1_tile(b, t)
            store_products(t, value * joined(1, b, t, load_b), value, way)
            return c

        lax.fori_loop(0, TILES, tile, 0, unroll=TILES)
        summed(b, res_l, way)

    blocks_of(tensor)

    s0 = field(res_l, 6)
    s1 = [field(res_l, k) for k in range(3)]
    pairs = ((0, 0), (1, 1), (2, 2), (0, 1), (0, 2), (1, 2))
    corr = []
    for a, b in pairs:
        value = s0 * xi[a] * xi[b] - xi[a] * s1[b] - xi[b] * s1[a] + field(res_l, 8 + 8 * a + b)
        corr.append((2.0 if a == b else 0.0) + SLOPE * value)
    scale = mass * press
    for k in range(6):
        pack = packed(scale * corr[k])
        for p in range(HALF):
            pack_c[p, k : k + 1, :] = pack[p : p + 1]
    for p in range(HALF):
        pack_c[p, 6:8, :] = jnp.zeros((2, 128), F32)
    c_go()
    for p in range(HALF):
        reg_c[here, p] = pack_c[p]

    def masses(b, way):
        def tile(t, c):
            value = far1_tile(b, t)
            fm = far[pl.ds((b * TILES + t) * 8 + 6, 1), :]
            store_products(t, value * fm, value, way)
            return c

        lax.fori_loop(0, TILES, tile, 0, unroll=TILES)
        summed(b, res_m, way)

    blocks_of(masses)

    a0 = field(res_m, 6)
    a1 = [field(res_m, k) for k in range(3)]
    v1 = [field(res_m, 3 + k) for k in range(3)]
    at = ((0, 3, 4), (3, 1, 5), (4, 5, 2))
    grad = [a0 * xi[a] - a1[a] for a in range(3)]
    pull = []
    heat = None
    for a in range(3):
        row = [corr[at[a][b]] for b in range(3)]
        pull.append(press * (row[0] * grad[0] + row[1] * grad[1] + row[2] * grad[2]))
        for b in range(3):
            work = vi[a] * grad[b] - v1[a] * xi[b] + field(res_m, 8 + 8 * b + 3 + a)
            term = row[b] * work
            heat = term if heat is None else heat + term
    energy = own_e[0:B] + STEP_DT * SLOPE * (live * press * heat)

    c_in()

    @pl.when(dom == 0)
    def _():
        for d in range(G):
            for p in range(HALF):
                reg_c[d, p] = zero

    @pl.when(dom == D - 1)
    def _():
        for d in range(G):
            for p in range(HALF):
                reg_c[2 * G + d, p] = zero

    def momentum(b, way):
        def tile(t, c):
            store_products(t, joined(1, b, t, load_c), far1_tile(b, t), way)
            return c

        lax.fori_loop(0, TILES, tile, 0, unroll=TILES)
        summed(b, res_q, way)

    blocks_of(momentum)

    for a in range(3):
        far_sum = None
        for b in range(3):
            k = at[a][b]
            term = field(res_q, k) * xi[b] - field(res_q, 8 + 8 * b + k)
            far_sum = term if far_sum is None else far_sum + term
        accel = (-SLOPE) * live * (pull[a] + far_sum)
        velocity = own_field(far, 3 + a) + STEP_DT * accel
        position = own_field(far, a) + STEP_DT * velocity
        out_ref[pl.ds((a) * B, B), :] = position[:, 0:W]
        out_ref[pl.ds((3 + a) * B, B), :] = velocity[:, 0:W]
    out_ref[pl.ds((6) * B, B), :] = own_e[B : 2 * B, 0:W]
    out_ref[pl.ds((7) * B, B), :] = smooth[:, 0:W]
    out_ref[pl.ds((8) * B, B), :] = energy[:, 0:W]

    meta_out()
    a_out()
    b_out()
    c_out()


def local(sizes, state, counts, neighbours, new_place):
    D, G = sizes
    blocks, _, width = state.shape
    NBR = neighbours.shape[1]
    tiles = (NBR + 2) // 2
    half = blocks // 2
    vmem = pl.BlockSpec(memory_space=pltpu.VMEM)
    smem = pl.BlockSpec(memory_space=pltpu.SMEM)
    sems = pltpu.SemaphoreType.DMA((3 * G,))
    moved, rho = pl.pallas_call(
        functools.partial(kernel, (D, G, NBR)),
        out_shape=(
            jax.ShapeDtypeStruct((9 * blocks, width), F32),
            jax.ShapeDtypeStruct((blocks, width), F32),
        ),
        in_specs=[vmem, vmem, smem, smem],
        out_specs=(vmem, vmem),
        scratch_shapes=[
            pltpu.VMEM((8, 128), jnp.int32),
            pltpu.VMEM((half + 1, 8, 128), F32),
            pltpu.VMEM((8, 128), F32),
            pltpu.VMEM((half, 8, 128), F32),
            pltpu.VMEM((3 * G, 8, 128), jnp.int32),
            pltpu.VMEM((3 * G + 1, half + 1, 8, 128), F32),
            pltpu.VMEM((3 * G + 1, 8, 128), F32),
            pltpu.VMEM((3 * G + 1, half, 8, 128), F32),
            pltpu.VMEM((2, 8, 128), jnp.int32),
            pltpu.SMEM((2, 8, 128), jnp.int32),
            pltpu.VMEM((blocks * tiles * 8, 128), F32),
            pltpu.VMEM((blocks * tiles * 8, 128), F32),
            pltpu.VMEM((4, width, 128), F32),
            pltpu.VMEM((blocks, width, 128), F32),
            pltpu.VMEM((blocks, width, tiles * 128), F32),
            pltpu.VMEM((SPLITS, blocks, width, tiles * 128), BF16),
            pltpu.VMEM((16, 128), F32),
            pltpu.VMEM((8, 128), F32),
            pltpu.VMEM((blocks * 32, 128), F32),
            pltpu.VMEM((blocks * 32, 128), F32),
            pltpu.VMEM((blocks * 32, 128), F32),
            pltpu.VMEM((4, SPLITS * 32, tiles * 128), BF16),
            pltpu.SemaphoreType.DMA,
        ]
        + [sems] * 8,
        compiler_params=pltpu.CompilerParams(
            collective_id=0, has_side_effects=True, vmem_limit_bytes=40 * 2**20
        ),
    )(
        jnp.transpose(state, (1, 0, 2)).reshape(9 * blocks, width),
        neighbours,
        counts,
        new_place,
    )
    return (jnp.transpose(moved.reshape(9, blocks, width), (1, 0, 2)), rho)


def solution(mesh):
    sizes = (mesh.shape["dom"], mesh.shape["seg"])
    both = ("dom", "seg")
    return jax.shard_map(
        functools.partial(local, sizes),
        mesh=mesh,
        in_specs=(P(both, None, None), P(both), P(both, None), P(both)),
        out_specs=(P(both, None, None), P(both, None)),
        check_vma=False,
    )
```

```python
import functools
import math

import jax
import jax.numpy as jnp
from jax import lax
from jax.experimental import pallas as pl
from jax.experimental.pallas import tpu as pltpu
from jax.sharding import PartitionSpec as P

SIGMA = 21.0 / (16.0 * math.pi)
SLOPE = -5.0 * 32.0 * SIGMA
GAMMA_LESS = 2.0 / 3.0
STEP_DT = 0.1
MESH = pl.DeviceIdType.MESH
F32 = jnp.float32
BF16 = jnp.bfloat16
SPLITS = 3
TINY = 1e-36


def split(value):
    parts = []
    for k in range(SPLITS):
        part = value.astype(BF16)
        parts.append(part)
        if k + 1 < SPLITS:
            value = value - part.astype(F32)
    return parts


def kernel(
    dims,
    state_hbm,
    nb_hbm,
    counts_hbm,
    place_hbm,
    out_ref,
    rho_ref,
    meta,
    pack_a,
    pack_b,
    pack_c,
    reg_m,
    reg_a,
    reg_b,
    reg_c,
    table,
    table_smem,
    far,
    far1,
    own_wide,
    centres,
    accs,
    smooth_wide,
    dists,
    weights,
    own_e,
    sums,
    res_l,
    res_m,
    res_q,
    moment,
    state_ref,
    nb_ref,
    counts_ref,
    place_ref,
    fetch_sem,
    copy_sem,
    send_m,
    recv_m,
    send_a,
    recv_a,
    send_b,
    recv_b,
    send_c,
    recv_c,
):
    D, G, NBR = dims
    B = 8
    HALF = B // 2
    W = 64
    SLAB = G * B
    TILES = (NBR + 2) // 2
    SELF, PAD, PLACE, COUNT, TABLE0 = NBR, NBR + 1, 28, 29, 64
    dom = lax.axis_index("dom")
    seg = lax.axis_index("seg")

    def wrapped(value, size):
        return value & (size - 1) if size & (size - 1) == 0 else lax.rem(value, size)

    def target(delta, o):
        return (wrapped(dom + delta + D, D), wrapped(seg + o, G))

    steps = (6, 2, 5, 7, 4, 1, 3, 0) if G == 8 else tuple(range(G))
    away = 2 * (dom & 1) - 1

    def others(action):
        for o in steps:
            action(away, o)
        for o in steps:
            action(-away, o)

    def group(action):
        for o in steps:
            if o:
                action(0, o)

    def each_peer(action):
        others(action)
        group(action)

    barrier = pltpu.get_barrier_semaphore()

    def greet(delta, o):
        pl.semaphore_signal(barrier, inc=1, device_id=target(delta, o), device_id_type=MESH)

    each_peer(greet)
    fetches = [
        pltpu.make_async_copy(src, dst, fetch_sem.at[k])
        for k, (src, dst) in enumerate(
            (
                (place_hbm, place_ref),
                (counts_hbm, counts_ref),
                (nb_hbm, nb_ref),
                (state_hbm, state_ref),
            )
        )
    ]
    for fetch in fetches:
        fetch.start()
    for fetch in fetches:
        fetch.wait()

    rows = lax.broadcasted_iota(jnp.int32, (B, 128), 0)
    lanes = lax.broadcasted_iota(jnp.int32, (B, 128), 1)
    low = lanes < W

    note = jnp.where(lanes == SELF, SLAB + seg * B + rows, 0)
    note = jnp.where(lanes == PAD, 3 * SLAB, note)
    for b in range(B):
        mine = rows == b
        note = jnp.where(mine & (lanes == PLACE), place_ref[b], note)
        note = jnp.where(mine & (lanes == COUNT), counts_ref[b], note)
        note = jnp.where((rows == 0) & (lanes == TABLE0 + seg * B + b), place_ref[b], note)
    meta[...] = note
    meta[:, 0:NBR] = nb_ref[...]
    for p in range(HALF):
        pair = jnp.concatenate(
            [state_ref[pl.ds(q, 8, stride=B), :] for q in (p, p + HALF)], axis=1
        )
        limit = jnp.where(low, counts_ref[p], counts_ref[p + HALF] + W)
        pack_a[p] = jnp.where((rows == 6) & (lanes >= limit), 0.0, pair)
    for k, f in enumerate((8, 6)):
        pack_a[HALF, k * HALF : k * HALF + HALF] = jnp.concatenate(
            [state_ref[f * B + h * HALF : f * B + h * HALF + HALF, :] for h in (0, 1)], axis=1
        )

    pl.semaphore_wait(barrier, 3 * G - 1)

    def sent(src, dst, send_sem, recv_sem, each_peer=each_peer):
        def make(delta, o):
            slot = (1 - delta) * G + seg
            return pltpu.make_async_remote_copy(
                src_ref=src(delta),
                dst_ref=dst(slot, delta),
                send_sem=send_sem.at[(1 + delta) * G + o],
                recv_sem=recv_sem.at[slot],
                device_id=target(delta, o),
                device_id_type=MESH,
            )

        def take(delta, o):
            slot = (1 + delta) * G + wrapped(seg + o, G)
            return pltpu.make_async_remote_copy(
                src_ref=src(delta),
                dst_ref=dst(slot, delta),
                send_sem=send_sem.at[(1 + delta) * G + o],
                recv_sem=recv_sem.at[slot],
                device_id=target(delta, o),
                device_id_type=MESH,
            )

        return (
            lambda: each_peer(lambda delta, o: make(delta, o).start()),
            lambda: each_peer(lambda delta, o: take(delta, o).wait_recv()),
            lambda: each_peer(lambda delta, o: make(delta, o).wait_send()),
        )

    near_go, near_in, near_out = sent(
        lambda d: meta, lambda s, d: reg_m.at[s], send_m, recv_m, group
    )
    wide_go, wide_in, wide_out = sent(
        lambda d: meta, lambda s, d: reg_m.at[s], send_m, recv_m, others
    )
    a_go, a_in, a_out = sent(
        lambda d: pack_a if type(d) is int else pack_a.at[0:HALF],
        lambda s, d: reg_a.at[s] if type(d) is int else reg_a.at[s, 0:HALF],
        send_a,
        recv_a,
    )
    b_go, b_in, b_out = sent(lambda d: pack_b, lambda s, d: reg_b.at[s], send_b, recv_b)
    c_go, c_in, c_out = sent(
        lambda d: pack_c.at[:, 0:6], lambda s, d: reg_c.at[s, :, 0:6], send_c, recv_c
    )

    near_go()
    a_go()
    wide_go()

    here = G + seg
    reg_m[here] = meta[...]
    reg_a[here] = pack_a[...]
    none = 3 * G
    zero = jnp.zeros((8, 128), F32)
    reg_b[none] = zero
    for p in range(HALF):
        reg_a[none, p] = zero
        reg_c[none, p] = zero
    reg_a[none, HALF] = zero

    near_in()
    lists = jnp.zeros((B, 128), jnp.int32)
    notes = [reg_m[G + d] for d in range(G)]
    places = [jnp.broadcast_to(note[:, PLACE : PLACE + 1], (B, 128)) for note in notes]
    for b in range(B):
        found = jnp.zeros((B, 128), jnp.int32)
        for d in range(G):
            found = found + jnp.where(places[d] == seg * B + b, notes[d], 0)
        for shift in (4, 2, 1):
            found = found + pltpu.roll(found, shift, 0)
        lists = jnp.where(rows == b, found, lists)
    inside = jnp.clip(lists, 0, 3 * SLAB)
    half = (inside >> 2) & 1
    table[0] = (((inside >> 3) * (HALF + 1) + (inside & 3)) << 1) | half
    live = jnp.where(lanes < jnp.broadcast_to(lists[:, COUNT : COUNT + 1], (B, 128)), 1.0, 0.0)

    def to_smem(which):
        return pltpu.make_async_copy(table.at[which], table_smem.at[which], copy_sem)

    to_smem(0).start()
    to_smem(0).wait()

    a_in()

    @pl.when(dom == 0)
    def _():
        for d in range(G):
            for p in range(HALF):
                reg_a[d, p] = zero

    @pl.when(dom == D - 1)
    def _():
        for d in range(G):
            for p in range(HALF):
                reg_a[2 * G + d, p] = zero

    def joined(which, b, t, load):
        even, odd = table_smem[which, b, 2 * t], table_smem[which, b, 2 * t + 1]
        left, right = load(even >> 1), load(odd >> 1)
        left = pltpu.roll(left, (even & 1) * W, 1)
        right = pltpu.roll(right, W - (odd & 1) * W, 1)
        mask = low if left.shape[0] == B else low[0:1]
        return jnp.where(mask, left, right)

    def load_a(tile):
        return reg_a[lax.div(tile, HALF + 1), lax.rem(tile, HALF + 1)]

    def load_b(row):
        return reg_b[row >> 2, pl.ds(row & 3, 1), :]

    def load_c(tile):
        return reg_c[tile >> 2, tile & 3]

    for b in range(B):
        own = joined(0, b, TILES - 1, load_a)
        where_own = table_smem[0, b, SELF]
        dev, pair = lax.div(where_own >> 1, HALF + 1), lax.rem(where_own >> 1, HALF + 1)
        shift = (where_own & 1) * W
        own_e[b : b + 1, :] = pltpu.roll(reg_a[dev, HALF, pl.ds(pair, 1), :], shift, 1)
        own_e[B + b : B + b + 1, :] = pltpu.roll(
            reg_a[dev, HALF, pl.ds(HALF + pair, 1), :], shift, 1
        )
        centre = jnp.sum(jnp.where(low, own, 0.0), axis=1, keepdims=True) * (1.0 / W)
        centre = jnp.where(rows < 6, jnp.broadcast_to(centre, (B, 128)), 0.0)
        centres[b] = centre
        turned = jnp.transpose(own)[0:W]
        for k, field in enumerate((0, 1, 2, 7)):
            own_wide[b, k] = jnp.broadcast_to(turned[:, field : field + 1], (W, 128))
        smooth_wide[b] = own_wide[b, 3]
        own_wide[b, 3] = 0.5 / own_wide[b, 3]

    def density(b, c):
        centre = centres[b]

        def tile(t, acc):
            value = joined(0, b, t, load_a)
            far[pl.ds(pl.multiple_of((b * TILES + t) * 8, 8), 8), :] = value
            far1[pl.ds(pl.multiple_of((b * TILES + t) * 8, 8), 8), :] = jnp.where(
                rows == 6, 1.0, value - centre
            )
            fx, fy, fz = value[0:1], value[1:2], value[2:3]
            fm = value[6:7]
            at = pl.ds(pl.multiple_of(t * 128, 128), 128)
            new = []
            for g in range(W // 16):
                part = pl.ds(g * 16, 16)
                dx = own_wide[b, 0, part, :] - fx
                dy = own_wide[b, 1, part, :] - fy
                dz = own_wide[b, 2, part, :] - fz
                square = jnp.maximum(dx * dx + dy * dy + dz * dz, TINY)
                dist = square * lax.rsqrt(square)
                q = dist * own_wide[b, 3, part, :]
                shell = jnp.maximum(1.0 - q, 0.0)
                shell = shell * shell
                kern = shell * shell * (1.0 + 4.0 * q)
                new.append(acc[g * 16 : g * 16 + 16] + kern * fm)
                dists[b, part, at] = dist
            return jnp.concatenate(new, axis=0)

        accs[b] = lax.fori_loop(0, TILES, tile, jnp.zeros((W, 128), F32), unroll=TILES)
        return c

    lax.fori_loop(0, B, density, 0)
    for b in range(B):
        sums[b : b + 1, 0:W] = jnp.sum(jnp.transpose(accs[b]), axis=0, keepdims=True)

    def own_field(ref, k):
        return ref[pl.ds((TILES - 1) * 8 + k, B, stride=TILES * 8), :]

    mass, smooth = own_field(far, 6), own_field(far, 7)
    xi = [own_field(far1, k) for k in range(3)]
    vi = [own_field(far1, 3 + k) for k in range(3)]
    rho = SIGMA / (smooth * smooth * smooth) * sums[...] + (1.0 - live)
    rho = jnp.where(low, rho, 1.0)
    vol = mass / rho
    press = GAMMA_LESS * own_e[0:B] / rho
    rho_ref[...] = rho[:, 0:W]

    def packed(value):
        return jnp.concatenate([value[0:HALF, 0:W], value[HALF:B, 0:W]], axis=1)

    pack_b[0:HALF, :] = packed(vol)
    pack_b[HALF:B, :] = jnp.zeros((HALF, 128), F32)
    b_go()
    wide_in()
    spread = []
    for q in range(3):
        total = reg_m[q * G, 0:1, :]
        for d in range(1, G):
            total = total + reg_m[q * G + d, 0:1, :]
        total = jnp.broadcast_to(total, (B, 128))
        spread.append(jnp.where(low, pltpu.roll(total, W, 1), total))
    first = jnp.where(low, spread[0], spread[1]) if SLAB == W else None
    if SLAB == W:
        inside = lists & 127
        placed = jnp.where(
            lists < 128,
            jnp.take_along_axis(first, inside, axis=1, mode="promise_in_bounds"),
            jnp.take_along_axis(spread[2], inside, axis=1, mode="promise_in_bounds"),
        )
        moved = jnp.where(lists < 3 * SLAB, (lists & (-SLAB)) + placed, lists)
    else:
        moved = lists
        inside = lists & (SLAB - 1)
        for q in range(3):
            got = jnp.take_along_axis(spread[q], inside, axis=1, mode="promise_in_bounds")
            moved = jnp.where((lists >= q * SLAB) & (lists < (q + 1) * SLAB), q * SLAB + got, moved)
    moved = jnp.clip(moved, 0, 3 * SLAB)
    table[1] = (((moved >> 3) * HALF + (moved & 3)) << 1) | ((moved >> 2) & 1)
    to_smem(1).start()
    to_smem(1).wait()
    reg_b[here] = pack_b[...]

    def blocks_of(body):
        def several(i, c):
            for k in range(4):
                body(i * 4 + k, k)
            return c

        lax.fori_loop(0, B // 4, several, 0)

    def store_moment(k, t, value, way):
        at = pl.ds(pl.multiple_of(t * 128, 128), 128)
        for s, piece in enumerate(split(value)):
            moment[way, pl.ds(s * 32 + k * 16, 16), at] = piece

    def store_products(t, tile, by, way):
        store_moment(0, t, jnp.concatenate([tile, tile * by[0:1]], axis=0), way)
        store_moment(1, t, jnp.concatenate([tile * by[1:2], tile * by[2:3]], axis=0), way)

    def summed(b, out, way):
        total = None
        for k in range(SPLITS):
            got = lax.dot_general(
                moment[way, 0 : 32 * (SPLITS - k), :],
                weights[k, b],
                (((1,), (1,)), ((), ())),
                preferred_element_type=F32,
            )
            for s in range(SPLITS - k):
                piece = got[32 * s : 32 * s + 32]
                total = piece if total is None else total + piece
        out[pl.ds(pl.multiple_of(b * 32, 32), 32), 0:W] = total

    def far1_tile(b, t):
        return far1[pl.ds(pl.multiple_of((b * TILES + t) * 8, 8), 8), :]

    def field(ref, k):
        return ref[pl.ds(k, B, stride=32), :]

    def slopes(b, c):
        def tile(t, c):
            fh = far[pl.ds((b * TILES + t) * 8 + 7, 1), :]
            at = pl.ds(pl.multiple_of(t * 128, 128), 128)
            for g in range(W // 16):
                part = pl.ds(g * 16, 16)
                inv = 1.0 / (smooth_wide[b, part, :] + fh)
                shell = jnp.maximum(1.0 - dists[b, part, at] * inv, 0.0) * inv
                shell2 = shell * shell
                factor = (shell * (inv * inv)) * shell2
                for k, piece in enumerate(split(factor)):
                    weights[k, b, part, at] = piece
            return c

        lax.fori_loop(0, TILES, tile, 0, unroll=TILES)
        return c

    lax.fori_loop(0, B, slopes, 0)

    near_out()
    a_out()
    wide_out()
    b_in()

    @pl.when(dom == 0)
    def _():
        for d in range(G):
            reg_b[d] = zero

    @pl.when(dom == D - 1)
    def _():
        for d in range(G):
            reg_b[2 * G + d] = zero

    def tensor(b, way):
        def tile(t, c):
            value = far1_tile(b, t)
            store_products(t, value * joined(1, b, t, load_b), value, way)
            return c

        lax.fori_loop(0, TILES, tile, 0, unroll=TILES)
        summed(b, res_l, way)

    blocks_of(tensor)

    s0 = field(res_l, 6)
    s1 = [field(res_l, k) for k in range(3)]
    pairs = ((0, 0), (1, 1), (2, 2), (0, 1), (0, 2), (1, 2))
    corr = []
    for a, b in pairs:
        value = s0 * xi[a] * xi[b] - xi[a] * s1[b] - xi[b] * s1[a] + field(res_l, 8 + 8 * a + b)
        corr.append((2.0 if a == b else 0.0) + SLOPE * value)
    scale = mass * press
    for k in range(6):
        pack = packed(scale * corr[k])
        for p in range(HALF):
            pack_c[p, k : k + 1, :] = pack[p : p + 1]
    for p in range(HALF):
        pack_c[p, 6:8, :] = jnp.zeros((2, 128), F32)
    c_go()
    for p in range(HALF):
        reg_c[here, p] = pack_c[p]

    def masses(b, way):
        def tile(t, c):
            value = far1_tile(b, t)
            fm = far[pl.ds((b * TILES + t) * 8 + 6, 1), :]
            store_products(t, value * fm, value, way)
            return c

        lax.fori_loop(0, TILES, tile, 0, unroll=TILES)
        summed(b, res_m, way)

    blocks_of(masses)

    a0 = field(res_m, 6)
    a1 = [field(res_m, k) for k in range(3)]
    v1 = [field(res_m, 3 + k) for k in range(3)]
    at = ((0, 3, 4), (3, 1, 5), (4, 5, 2))
    grad = [a0 * xi[a] - a1[a] for a in range(3)]
    pull = []
    heat = None
    for a in range(3):
        row = [corr[at[a][b]] for b in range(3)]
        pull.append(press * (row[0] * grad[0] + row[1] * grad[1] + row[2] * grad[2]))
        for b in range(3):
            work = vi[a] * grad[b] - v1[a] * xi[b] + field(res_m, 8 + 8 * b + 3 + a)
            term = row[b] * work
            heat = term if heat is None else heat + term
    energy = own_e[0:B] + STEP_DT * SLOPE * (live * press * heat)

    b_out()
    c_out()
    c_in()

    @pl.when(dom == 0)
    def _():
        for d in range(G):
            for p in range(HALF):
                reg_c[d, p] = zero

    @pl.when(dom == D - 1)
    def _():
        for d in range(G):
            for p in range(HALF):
                reg_c[2 * G + d, p] = zero

    def momentum(b, way):
        def tile(t, c):
            store_products(t, joined(1, b, t, load_c), far1_tile(b, t), way)
            return c

        lax.fori_loop(0, TILES, tile, 0, unroll=TILES)
        summed(b, res_q, way)

    blocks_of(momentum)

    for a in range(3):
        far_sum = None
        for b in range(3):
            k = at[a][b]
            term = field(res_q, k) * xi[b] - field(res_q, 8 + 8 * b + k)
            far_sum = term if far_sum is None else far_sum + term
        accel = (-SLOPE) * live * (pull[a] + far_sum)
        velocity = own_field(far, 3 + a) + STEP_DT * accel
        position = own_field(far, a) + STEP_DT * velocity
        out_ref[pl.ds((a) * B, B), :] = position[:, 0:W]
        out_ref[pl.ds((3 + a) * B, B), :] = velocity[:, 0:W]
    out_ref[pl.ds((6) * B, B), :] = own_e[B : 2 * B, 0:W]
    out_ref[pl.ds((7) * B, B), :] = smooth[:, 0:W]
    out_ref[pl.ds((8) * B, B), :] = energy[:, 0:W]


def local(sizes, state, counts, neighbours, new_place):
    D, G = sizes
    blocks, _, width = state.shape
    NBR = neighbours.shape[1]
    tiles = (NBR + 2) // 2
    half = blocks // 2
    vmem = pl.BlockSpec(memory_space=pltpu.VMEM)
    hbm = pl.BlockSpec(memory_space=pltpu.HBM)
    sems = pltpu.SemaphoreType.DMA((3 * G,))
    moved, rho = pl.pallas_call(
        functools.partial(kernel, (D, G, NBR)),
        out_shape=(
            jax.ShapeDtypeStruct((9 * blocks, width), F32),
            jax.ShapeDtypeStruct((blocks, width), F32),
        ),
        in_specs=[hbm] * 4,
        out_specs=(vmem, vmem),
        scratch_shapes=[
            pltpu.VMEM((8, 128), jnp.int32),
            pltpu.VMEM((half + 1, 8, 128), F32),
            pltpu.VMEM((8, 128), F32),
            pltpu.VMEM((half, 8, 128), F32),
            pltpu.VMEM((3 * G, 8, 128), jnp.int32),
            pltpu.VMEM((3 * G + 1, half + 1, 8, 128), F32),
            pltpu.VMEM((3 * G + 1, 8, 128), F32),
            pltpu.VMEM((3 * G + 1, half, 8, 128), F32),
            pltpu.VMEM((2, 8, 128), jnp.int32),
            pltpu.SMEM((2, 8, 128), jnp.int32),
            pltpu.VMEM((blocks * tiles * 8, 128), F32),
            pltpu.VMEM((blocks * tiles * 8, 128), F32),
            pltpu.VMEM((blocks, 4, width, 128), F32),
            pltpu.VMEM((blocks, 8, 128), F32),
            pltpu.VMEM((blocks, width, 128), F32),
            pltpu.VMEM((blocks, width, 128), F32),
            pltpu.VMEM((blocks, width, tiles * 128), F32),
            pltpu.VMEM((SPLITS, blocks, width, tiles * 128), BF16),
            pltpu.VMEM((16, 128), F32),
            pltpu.VMEM((8, 128), F32),
            pltpu.VMEM((blocks * 32, 128), F32),
            pltpu.VMEM((blocks * 32, 128), F32),
            pltpu.VMEM((blocks * 32, 128), F32),
            pltpu.VMEM((4, SPLITS * 32, tiles * 128), BF16),
            pltpu.VMEM((9 * blocks, width), F32),
            pltpu.VMEM((blocks, NBR), jnp.int32),
            pltpu.SMEM((blocks,), jnp.int32),
            pltpu.SMEM((blocks,), jnp.int32),
            pltpu.SemaphoreType.DMA((4,)),
            pltpu.SemaphoreType.DMA,
        ]
        + [sems] * 8,
        compiler_params=pltpu.CompilerParams(
            collective_id=0, has_side_effects=True, vmem_limit_bytes=56 * 2**20
        ),
    )(
        jnp.transpose(state, (1, 0, 2)).reshape(9 * blocks, width),
        neighbours,
        counts,
        new_place,
    )
    return (jnp.transpose(moved.reshape(9, blocks, width), (1, 0, 2)), rho)


def solution(mesh):
    sizes = (mesh.shape["dom"], mesh.shape["seg"])
    both = ("dom", "seg")
    return jax.shard_map(
        functools.partial(local, sizes),
        mesh=mesh,
        in_specs=(P(both, None, None), P(both), P(both, None), P(both)),
        out_specs=(P(both, None, None), P(both, None)),
        check_vma=False,
    )
```

```python
import functools
import math

import jax
import jax.numpy as jnp
from jax import lax
from jax.experimental import pallas as pl
from jax.experimental.pallas import tpu as pltpu
from jax.sharding import PartitionSpec as P

SIGMA = 21.0 / (16.0 * math.pi)
SLOPE = -5.0 * 32.0 * SIGMA
GAMMA_LESS = 2.0 / 3.0
STEP_DT = 0.1
MESH = pl.DeviceIdType.MESH
F32 = jnp.float32
BF16 = jnp.bfloat16
SPLITS = 3
TINY = 1e-36


def split(value):
    parts = []
    for k in range(SPLITS):
        part = value.astype(BF16)
        parts.append(part)
        if k + 1 < SPLITS:
            value = value - part.astype(F32)
    return parts


def kernel(
    dims,
    state_hbm,
    nb_hbm,
    counts_hbm,
    place_hbm,
    out_ref,
    rho_ref,
    meta,
    pack_a,
    pack_b,
    pack_c,
    reg_m,
    reg_a,
    reg_b,
    reg_c,
    table,
    table_smem,
    far,
    far1,
    own_wide,
    centres,
    accs,
    smooth_wide,
    dists,
    weights,
    own_e,
    sums,
    res_l,
    res_m,
    res_q,
    moment,
    state_ref,
    nb_ref,
    counts_ref,
    place_ref,
    fetch_sem,
    copy_sem,
    send_m,
    recv_m,
    send_a,
    recv_a,
    send_b,
    recv_b,
    send_c,
    recv_c,
):
    D, G, NBR = dims
    B = 8
    HALF = B // 2
    W = 64
    SLAB = G * B
    TILES = (NBR + 2) // 2
    SELF, PAD, PLACE, COUNT, TABLE0 = NBR, NBR + 1, 28, 29, 64
    dom = lax.axis_index("dom")
    seg = lax.axis_index("seg")

    def wrapped(value, size):
        return value & (size - 1) if size & (size - 1) == 0 else lax.rem(value, size)

    def target(delta, o):
        return (wrapped(dom + delta + D, D), wrapped(seg + o, G))

    steps = (6, 2, 5, 7, 4, 1, 3, 0) if G == 8 else tuple(range(G))
    away = 2 * (dom & 1) - 1

    def others(action):
        for o in steps:
            action(away, o)
        for o in steps:
            action(-away, o)

    def group(action):
        for o in steps:
            if o:
                action(0, o)

    def each_peer(action):
        others(action)
        group(action)

    barrier = pltpu.get_barrier_semaphore()

    def greet(delta, o):
        pl.semaphore_signal(barrier, inc=1, device_id=target(delta, o), device_id_type=MESH)

    each_peer(greet)
    fetches = [
        pltpu.make_async_copy(src, dst, fetch_sem.at[k])
        for k, (src, dst) in enumerate(
            (
                (place_hbm, place_ref),
                (counts_hbm, counts_ref),
                (nb_hbm, nb_ref),
                (state_hbm, state_ref),
            )
        )
    ]
    for fetch in fetches:
        fetch.start()
    for fetch in fetches:
        fetch.wait()

    rows = lax.broadcasted_iota(jnp.int32, (B, 128), 0)
    lanes = lax.broadcasted_iota(jnp.int32, (B, 128), 1)
    low = lanes < W

    note = jnp.where(lanes == SELF, SLAB + seg * B + rows, 0)
    note = jnp.where(lanes == PAD, 3 * SLAB, note)
    for b in range(B):
        mine = rows == b
        note = jnp.where(mine & (lanes == PLACE), place_ref[b], note)
        note = jnp.where(mine & (lanes == COUNT), counts_ref[b], note)
        note = jnp.where((rows == 0) & (lanes == TABLE0 + seg * B + b), place_ref[b], note)
    meta[...] = note
    meta[:, 0:NBR] = nb_ref[...]
    for p in range(HALF):
        pair = jnp.concatenate(
            [state_ref[pl.ds(q, 8, stride=B), :] for q in (p, p + HALF)], axis=1
        )
        limit = jnp.where(low, counts_ref[p], counts_ref[p + HALF] + W)
        pack_a[p] = jnp.where((rows == 6) & (lanes >= limit), 0.0, pair)
    for k, f in enumerate((8, 6)):
        pack_a[HALF, k * HALF : k * HALF + HALF] = jnp.concatenate(
            [state_ref[f * B + h * HALF : f * B + h * HALF + HALF, :] for h in (0, 1)], axis=1
        )

    pl.semaphore_wait(barrier, 3 * G - 1)

    def sent(src, dst, send_sem, recv_sem, each_peer=each_peer):
        def make(delta, o):
            slot = (1 - delta) * G + seg
            return pltpu.make_async_remote_copy(
                src_ref=src(delta),
                dst_ref=dst(slot, delta),
                send_sem=send_sem.at[(1 + delta) * G + o],
                recv_sem=recv_sem.at[slot],
                device_id=target(delta, o),
                device_id_type=MESH,
            )

        def take(delta, o):
            slot = (1 + delta) * G + wrapped(seg + o, G)
            return pltpu.make_async_remote_copy(
                src_ref=src(delta),
                dst_ref=dst(slot, delta),
                send_sem=send_sem.at[(1 + delta) * G + o],
                recv_sem=recv_sem.at[slot],
                device_id=target(delta, o),
                device_id_type=MESH,
            )

        return (
            lambda: each_peer(lambda delta, o: make(delta, o).start()),
            lambda: each_peer(lambda delta, o: take(delta, o).wait_recv()),
            lambda: each_peer(lambda delta, o: make(delta, o).wait_send()),
        )

    near_go, near_in, near_out = sent(
        lambda d: meta, lambda s, d: reg_m.at[s], send_m, recv_m, group
    )
    wide_go, wide_in, wide_out = sent(
        lambda d: meta, lambda s, d: reg_m.at[s], send_m, recv_m, others
    )
    a_go, a_in, a_out = sent(
        lambda d: pack_a if type(d) is int else pack_a.at[0:HALF],
        lambda s, d: reg_a.at[s] if type(d) is int else reg_a.at[s, 0:HALF],
        send_a,
        recv_a,
    )
    b_go, b_in, b_out = sent(lambda d: pack_b, lambda s, d: reg_b.at[s], send_b, recv_b)
    c_go, c_in, c_out = sent(
        lambda d: pack_c.at[:, 0:6], lambda s, d: reg_c.at[s, :, 0:6], send_c, recv_c
    )

    near_go()
    a_go()
    wide_go()

    here = G + seg
    reg_m[here] = meta[...]
    reg_a[here] = pack_a[...]
    none = 3 * G
    zero = jnp.zeros((8, 128), F32)
    reg_b[none] = zero
    for p in range(HALF):
        reg_a[none, p] = zero
        reg_c[none, p] = zero
    reg_a[none, HALF] = zero

    near_in()
    lists = jnp.zeros((B, 128), jnp.int32)
    notes = [reg_m[G + d] for d in range(G)]
    places = [jnp.broadcast_to(note[:, PLACE : PLACE + 1], (B, 128)) for note in notes]
    for b in range(B):
        found = jnp.zeros((B, 128), jnp.int32)
        for d in range(G):
            found = found + jnp.where(places[d] == seg * B + b, notes[d], 0)
        for shift in (4, 2, 1):
            found = found + pltpu.roll(found, shift, 0)
        lists = jnp.where(rows == b, found, lists)
    inside = jnp.clip(lists, 0, 3 * SLAB)
    half = (inside >> 2) & 1
    table[0] = (((inside >> 3) * (HALF + 1) + (inside & 3)) << 1) | half
    live = jnp.where(lanes < jnp.broadcast_to(lists[:, COUNT : COUNT + 1], (B, 128)), 1.0, 0.0)

    def to_smem(which):
        return pltpu.make_async_copy(table.at[which], table_smem.at[which], copy_sem)

    to_smem(0).start()
    to_smem(0).wait()

    a_in()

    @pl.when(dom == 0)
    def _():
        for d in range(G):
            for p in range(HALF):
                reg_a[d, p] = zero

    @pl.when(dom == D - 1)
    def _():
        for d in range(G):
            for p in range(HALF):
                reg_a[2 * G + d, p] = zero

    def joined(which, b, t, load):
        even, odd = table_smem[which, b, 2 * t], table_smem[which, b, 2 * t + 1]
        left, right = load(even >> 1), load(odd >> 1)
        left = pltpu.roll(left, (even & 1) * W, 1)
        right = pltpu.roll(right, W - (odd & 1) * W, 1)
        mask = low if left.shape[0] == B else low[0:1]
        return jnp.where(mask, left, right)

    def load_a(tile):
        return reg_a[lax.div(tile, HALF + 1), lax.rem(tile, HALF + 1)]

    def load_b(row):
        return reg_b[row >> 2, pl.ds(row & 3, 1), :]

    def load_c(tile):
        return reg_c[tile >> 2, tile & 3]

    for b in range(B):
        own = joined(0, b, TILES - 1, load_a)
        where_own = table_smem[0, b, SELF]
        dev, pair = lax.div(where_own >> 1, HALF + 1), lax.rem(where_own >> 1, HALF + 1)
        shift = (where_own & 1) * W
        own_e[b : b + 1, :] = pltpu.roll(reg_a[dev, HALF, pl.ds(pair, 1), :], shift, 1)
        own_e[B + b : B + b + 1, :] = pltpu.roll(
            reg_a[dev, HALF, pl.ds(HALF + pair, 1), :], shift, 1
        )
        centre = jnp.sum(jnp.where(low, own, 0.0), axis=1, keepdims=True) * (1.0 / W)
        centre = jnp.where(rows < 6, jnp.broadcast_to(centre, (B, 128)), 0.0)
        centres[b] = centre
        turned = jnp.transpose(own)[0:W]
        for k, field in enumerate((0, 1, 2, 7)):
            own_wide[b, k] = jnp.broadcast_to(turned[:, field : field + 1], (W, 128))
        smooth_wide[b] = own_wide[b, 3]
        own_wide[b, 3] = 0.5 / own_wide[b, 3]

    def density(b, c):
        centre = centres[b]

        def tile(t, acc):
            value = joined(0, b, t, load_a)
            far[pl.ds(pl.multiple_of((b * TILES + t) * 8, 8), 8), :] = value
            far1[pl.ds(pl.multiple_of((b * TILES + t) * 8, 8), 8), :] = jnp.where(
                rows == 6, 1.0, value - centre
            )
            fx, fy, fz = value[0:1], value[1:2], value[2:3]
            fm = value[6:7]
            at = pl.ds(pl.multiple_of(t * 128, 128), 128)
            new = []
            for g in range(W // 16):
                part = pl.ds(g * 16, 16)
                dx = own_wide[b, 0, part, :] - fx
                dy = own_wide[b, 1, part, :] - fy
                dz = own_wide[b, 2, part, :] - fz
                square = jnp.maximum(dx * dx + dy * dy + dz * dz, TINY)
                dist = square * lax.rsqrt(square)
                q = dist * own_wide[b, 3, part, :]
                shell = jnp.maximum(1.0 - q, 0.0)
                shell = shell * shell
                kern = shell * shell * (1.0 + 4.0 * q)
                new.append(acc[g * 16 : g * 16 + 16] + kern * fm)
                dists[b, part, at] = dist
            return jnp.concatenate(new, axis=0)

        accs[b] = lax.fori_loop(0, TILES, tile, jnp.zeros((W, 128), F32), unroll=TILES)
        return c

    lax.fori_loop(0, B, density, 0)
    for b in range(B):
        sums[b : b + 1, 0:W] = jnp.sum(jnp.transpose(accs[b]), axis=0, keepdims=True)

    def own_field(ref, k):
        return ref[pl.ds((TILES - 1) * 8 + k, B, stride=TILES * 8), :]

    mass, smooth = own_field(far, 6), own_field(far, 7)
    xi = [own_field(far1, k) for k in range(3)]
    vi = [own_field(far1, 3 + k) for k in range(3)]
    rho = SIGMA / (smooth * smooth * smooth) * sums[...] + (1.0 - live)
    rho = jnp.where(low, rho, 1.0)
    vol = mass / rho
    press = GAMMA_LESS * own_e[0:B] / rho
    rho_ref[...] = rho[:, 0:W]

    def packed(value):
        return jnp.concatenate([value[0:HALF, 0:W], value[HALF:B, 0:W]], axis=1)

    pack_b[0:HALF, :] = packed(vol)
    pack_b[HALF:B, :] = jnp.zeros((HALF, 128), F32)
    b_go()
    wide_in()
    spread = []
    for q in range(3):
        total = reg_m[q * G, 0:1, :]
        for d in range(1, G):
            total = total + reg_m[q * G + d, 0:1, :]
        total = jnp.broadcast_to(total, (B, 128))
        spread.append(jnp.where(low, pltpu.roll(total, W, 1), total))
    first = jnp.where(low, spread[0], spread[1]) if SLAB == W else None
    if SLAB == W:
        inside = lists & 127
        placed = jnp.where(
            lists < 128,
            jnp.take_along_axis(first, inside, axis=1, mode="promise_in_bounds"),
            jnp.take_along_axis(spread[2], inside, axis=1, mode="promise_in_bounds"),
        )
        moved = jnp.where(lists < 3 * SLAB, (lists & (-SLAB)) + placed, lists)
    else:
        moved = lists
        inside = lists & (SLAB - 1)
        for q in range(3):
            got = jnp.take_along_axis(spread[q], inside, axis=1, mode="promise_in_bounds")
            moved = jnp.where((lists >= q * SLAB) & (lists < (q + 1) * SLAB), q * SLAB + got, moved)
    moved = jnp.clip(moved, 0, 3 * SLAB)
    table[1] = (((moved >> 3) * HALF + (moved & 3)) << 1) | ((moved >> 2) & 1)
    to_smem(1).start()
    to_smem(1).wait()
    reg_b[here] = pack_b[...]

    def blocks_of(body):
        def several(i, c):
            for k in range(8):
                body(i * 8 + k, k)
            return c

        lax.fori_loop(0, B // 8, several, 0)

    def store_moment(k, t, value, way):
        at = pl.ds(pl.multiple_of(t * 128, 128), 128)
        for s, piece in enumerate(split(value)):
            moment[way, pl.ds(s * 32 + k * 16, 16), at] = piece

    def store_products(t, tile, by, way):
        store_moment(0, t, jnp.concatenate([tile, tile * by[0:1]], axis=0), way)
        store_moment(1, t, jnp.concatenate([tile * by[1:2], tile * by[2:3]], axis=0), way)

    def summed(b, out, way):
        total = None
        for k in range(SPLITS):
            got = lax.dot_general(
                moment[way, 0 : 32 * (SPLITS - k), :],
                weights[k, b],
                (((1,), (1,)), ((), ())),
                preferred_element_type=F32,
            )
            for s in range(SPLITS - k):
                piece = got[32 * s : 32 * s + 32]
                total = piece if total is None else total + piece
        out[pl.ds(pl.multiple_of(b * 32, 32), 32), 0:W] = total

    def far1_tile(b, t):
        return far1[pl.ds(pl.multiple_of((b * TILES + t) * 8, 8), 8), :]

    def field(ref, k):
        return ref[pl.ds(k, B, stride=32), :]

    def slopes(b, c):
        def tile(t, c):
            fh = far[pl.ds((b * TILES + t) * 8 + 7, 1), :]
            at = pl.ds(pl.multiple_of(t * 128, 128), 128)
            for g in range(W // 16):
                part = pl.ds(g * 16, 16)
                inv = 1.0 / (smooth_wide[b, part, :] + fh)
                shell = jnp.maximum(1.0 - dists[b, part, at] * inv, 0.0) * inv
                shell2 = shell * shell
                factor = (shell * (inv * inv)) * shell2
                for k, piece in enumerate(split(factor)):
                    weights[k, b, part, at] = piece
            return c

        lax.fori_loop(0, TILES, tile, 0, unroll=TILES)
        return c

    lax.fori_loop(0, B, slopes, 0)

    near_out()
    a_out()
    wide_out()
    b_in()

    @pl.when(dom == 0)
    def _():
        for d in range(G):
            reg_b[d] = zero

    @pl.when(dom == D - 1)
    def _():
        for d in range(G):
            reg_b[2 * G + d] = zero

    def tensor(b, way):
        def tile(t, c):
            value = far1_tile(b, t)
            store_products(t, value * joined(1, b, t, load_b), value, way)
            return c

        lax.fori_loop(0, TILES, tile, 0, unroll=TILES)
        summed(b, res_l, way)

    blocks_of(tensor)

    s0 = field(res_l, 6)
    s1 = [field(res_l, k) for k in range(3)]
    pairs = ((0, 0), (1, 1), (2, 2), (0, 1), (0, 2), (1, 2))
    corr = []
    for a, b in pairs:
        value = s0 * xi[a] * xi[b] - xi[a] * s1[b] - xi[b] * s1[a] + field(res_l, 8 + 8 * a + b)
        corr.append((2.0 if a == b else 0.0) + SLOPE * value)
    scale = mass * press
    for k in range(6):
        pack = packed(scale * corr[k])
        for p in range(HALF):
            pack_c[p, k : k + 1, :] = pack[p : p + 1]
    for p in range(HALF):
        pack_c[p, 6:8, :] = jnp.zeros((2, 128), F32)
    c_go()
    for p in range(HALF):
        reg_c[here, p] = pack_c[p]

    def masses(b, way):
        def tile(t, c):
            value = far1_tile(b, t)
            fm = far[pl.ds((b * TILES + t) * 8 + 6, 1), :]
            store_products(t, value * fm, value, way)
            return c

        lax.fori_loop(0, TILES, tile, 0, unroll=TILES)
        summed(b, res_m, way)

    blocks_of(masses)

    a0 = field(res_m, 6)
    a1 = [field(res_m, k) for k in range(3)]
    v1 = [field(res_m, 3 + k) for k in range(3)]
    at = ((0, 3, 4), (3, 1, 5), (4, 5, 2))
    grad = [a0 * xi[a] - a1[a] for a in range(3)]
    pull = []
    heat = None
    for a in range(3):
        row = [corr[at[a][b]] for b in range(3)]
        pull.append(press * (row[0] * grad[0] + row[1] * grad[1] + row[2] * grad[2]))
        for b in range(3):
            work = vi[a] * grad[b] - v1[a] * xi[b] + field(res_m, 8 + 8 * b + 3 + a)
            term = row[b] * work
            heat = term if heat is None else heat + term
    energy = own_e[0:B] + STEP_DT * SLOPE * (live * press * heat)

    b_out()
    c_out()
    c_in()

    @pl.when(dom == 0)
    def _():
        for d in range(G):
            for p in range(HALF):
                reg_c[d, p] = zero

    @pl.when(dom == D - 1)
    def _():
        for d in range(G):
            for p in range(HALF):
                reg_c[2 * G + d, p] = zero

    def momentum(b, way):
        def tile(t, c):
            store_products(t, joined(1, b, t, load_c), far1_tile(b, t), way)
            return c

        lax.fori_loop(0, TILES, tile, 0, unroll=TILES)
        summed(b, res_q, way)

    blocks_of(momentum)

    for a in range(3):
        far_sum = None
        for b in range(3):
            k = at[a][b]
            term = field(res_q, k) * xi[b] - field(res_q, 8 + 8 * b + k)
            far_sum = term if far_sum is None else far_sum + term
        accel = (-SLOPE) * live * (pull[a] + far_sum)
        velocity = own_field(far, 3 + a) + STEP_DT * accel
        position = own_field(far, a) + STEP_DT * velocity
        out_ref[pl.ds((a) * B, B), :] = position[:, 0:W]
        out_ref[pl.ds((3 + a) * B, B), :] = velocity[:, 0:W]
    out_ref[pl.ds((6) * B, B), :] = own_e[B : 2 * B, 0:W]
    out_ref[pl.ds((7) * B, B), :] = smooth[:, 0:W]
    out_ref[pl.ds((8) * B, B), :] = energy[:, 0:W]


def local(sizes, state, counts, neighbours, new_place):
    D, G = sizes
    blocks, _, width = state.shape
    NBR = neighbours.shape[1]
    tiles = (NBR + 2) // 2
    half = blocks // 2
    vmem = pl.BlockSpec(memory_space=pltpu.VMEM)
    hbm = pl.BlockSpec(memory_space=pltpu.HBM)
    sems = pltpu.SemaphoreType.DMA((3 * G,))
    moved, rho = pl.pallas_call(
        functools.partial(kernel, (D, G, NBR)),
        out_shape=(
            jax.ShapeDtypeStruct((9 * blocks, width), F32),
            jax.ShapeDtypeStruct((blocks, width), F32),
        ),
        in_specs=[hbm] * 4,
        out_specs=(vmem, vmem),
        scratch_shapes=[
            pltpu.VMEM((8, 128), jnp.int32),
            pltpu.VMEM((half + 1, 8, 128), F32),
            pltpu.VMEM((8, 128), F32),
            pltpu.VMEM((half, 8, 128), F32),
            pltpu.VMEM((3 * G, 8, 128), jnp.int32),
            pltpu.VMEM((3 * G + 1, half + 1, 8, 128), F32),
            pltpu.VMEM((3 * G + 1, 8, 128), F32),
            pltpu.VMEM((3 * G + 1, half, 8, 128), F32),
            pltpu.VMEM((2, 8, 128), jnp.int32),
            pltpu.SMEM((2, 8, 128), jnp.int32),
            pltpu.VMEM((blocks * tiles * 8, 128), F32),
            pltpu.VMEM((blocks * tiles * 8, 128), F32),
            pltpu.VMEM((blocks, 4, width, 128), F32),
            pltpu.VMEM((blocks, 8, 128), F32),
            pltpu.VMEM((blocks, width, 128), F32),
            pltpu.VMEM((blocks, width, 128), F32),
            pltpu.VMEM((blocks, width, tiles * 128), F32),
            pltpu.VMEM((SPLITS, blocks, width, tiles * 128), BF16),
            pltpu.VMEM((16, 128), F32),
            pltpu.VMEM((8, 128), F32),
            pltpu.VMEM((blocks * 32, 128), F32),
            pltpu.VMEM((blocks * 32, 128), F32),
            pltpu.VMEM((blocks * 32, 128), F32),
            pltpu.VMEM((8, SPLITS * 32, tiles * 128), BF16),
            pltpu.VMEM((9 * blocks, width), F32),
            pltpu.VMEM((blocks, NBR), jnp.int32),
            pltpu.SMEM((blocks,), jnp.int32),
            pltpu.SMEM((blocks,), jnp.int32),
            pltpu.SemaphoreType.DMA((4,)),
            pltpu.SemaphoreType.DMA,
        ]
        + [sems] * 8,
        compiler_params=pltpu.CompilerParams(
            collective_id=0, has_side_effects=True, vmem_limit_bytes=56 * 2**20
        ),
    )(
        jnp.transpose(state, (1, 0, 2)).reshape(9 * blocks, width),
        neighbours,
        counts,
        new_place,
    )
    return (jnp.transpose(moved.reshape(9, blocks, width), (1, 0, 2)), rho)


def solution(mesh):
    sizes = (mesh.shape["dom"], mesh.shape["seg"])
    both = ("dom", "seg")
    return jax.shard_map(
        functools.partial(local, sizes),
        mesh=mesh,
        in_specs=(P(both, None, None), P(both), P(both, None), P(both)),
        out_specs=(P(both, None, None), P(both, None)),
        check_vma=False,
    )
```
